32 devices in a mesh: parts: 2 (over y), hidden: 16 (over z, x, core).
Axes of the slice: x: 2, y: 2, z: 4, core: 2. Of those that a mesh axis runs over, the one named last changes fastest.
Arguments:
- tokens: bfloat16 [2, 128, 3072], P(None, ('parts', 'hidden')), parts along dimension 1, may hold values from -6 to 6
- route_ids: int32 [2, 128, 2], P(None, ('parts', 'hidden')), parts along dimension 1, may hold values from 0 to 7, all different within a row; in each aligned block of 4 rows (0 to 3, 4 to 7, ..., all dimensions but the last counted through in order) at most 2 rows name the same one
- route_weight: float32 [2, 128, 2], P(None, ('parts', 'hidden')), parts along dimension 1, may hold values from 0.1 to 0.9
- gate_weight: bfloat16 [3072, 65536], P(None, 'hidden'), may hold values from -0.109375 to 0.109375
- up_weight: bfloat16 [3072, 65536], P(None, 'hidden'), may hold values from -0.109375 to 0.109375
- down_weight: bfloat16 [65536, 3072], P('hidden'), may hold values from -0.0625 to 0.0625
Outputs:
- mixed: bfloat16 [2, 128, 3072], P(None, ('parts', 'hidden')), parts along dimension 1
The draws below stay inside these ranges and needn't reach their ends.
There are 2 independent parts, one for each index of `parts`. The reference program is written for one: setup_inputs(seed, part) draws one part's arguments, and reference() takes and returns one part's arrays. A program takes and returns all parts, laid end to end along the dimension named above; an argument that names none is the same for every part. Nothing has to cross between parts.
Inputs may be any that keep to these rules, and one draw needn't show every extreme that they name: `route_ids`: each row names 2 different experts. Among the rows of one device in one step (aligned blocks of 4 rows), at most 2 name the same expert, and in every draw some expert is named by exactly 2 of them.
All inputs are finite; a program needn't handle non-finite values.
Results may differ from the reference program's by a relative error of at most 0.009.
Values may be sent and summed in bfloat16 or wider, within the bound.
A program may use at most 192 MiB of HBM per device.

```python
import math
import jax
import jax.numpy as jnp
import numpy as np
from jax import lax

D = 3072
EXPERTS = 8
FF = 8192
TOP = 2
STEPS = 2
ROWS_DEV = 4
MOST = 2
ROWS = 64
N_HIDDEN = 16


def level_of(stream_key, extent, shards, smallest, largest):
    def one(dim, parts):
        steps = jax.random.uniform(jax.random.fold_in(jax.random.fold_in(stream_key, 6), dim), (parts,), jnp.float32, smallest / len(shards), largest / len(shards))
        return jnp.repeat(jnp.exp(steps), extent[dim] // parts).reshape((-1,) + (1,) * (len(extent) - dim - 1))

    factor_of = one(*shards[0])
    for cut in shards[1:]:
        factor_of = factor_of * one(*cut)
    return factor_of


def deal_out(key, own, number, rows, number_of, top, bound, slope):
    ranking = jax.random.permutation(key, number_of)
    packed, ordinary = portions_of(number_of, rows * top, bound, slope, True), portions_of(number_of, rows * top, bound, slope, False)
    places = jnp.arange(number_of)

    def named(tallies, rotation):
        used = int((tallies > 0).sum())
        fixed = max(1, used // 4)
        moved = fixed + (places - fixed + rotation * (used - fixed)) % max(1, number_of - fixed)
        return jnp.zeros((number_of,), jnp.int32).at[ranking[jnp.where(places < fixed, places, moved)]].set(jnp.asarray(tallies, jnp.int32))

    tallies = jnp.where(number % 4 == 0, named(packed, number // 4), named(ordinary, number - number // 4 - 1))
    mixed = jax.random.permutation(jax.random.fold_in(own, 3), number_of)
    source_of, taker = mixed[0:number_of // 2 * 2:2], mixed[1:number_of // 2 * 2:2]
    margin = jnp.minimum(tallies[source_of] - 1, bound - tallies[taker]) // 2
    margin = jnp.where((source_of == ranking[0]) | (taker == ranking[0]) | (tallies[taker] == 0), 0, jnp.maximum(margin, 0))
    moved = jax.random.randint(jax.random.fold_in(own, 4), (number_of // 2,), 0, 1 << 20) % (margin + 1)
    tallies = tallies.at[source_of].add(-moved).at[taker].add(moved)
    labels = jnp.searchsorted(jnp.cumsum(tallies), jnp.arange(rows * top), side="right").astype(jnp.int32)
    grid = labels.reshape(top, rows).T
    grid = grid[jax.random.permutation(jax.random.fold_in(own, 1), rows)]
    rotation = jax.random.randint(jax.random.fold_in(own, 2), (rows, 1), 0, top)
    return jnp.take_along_axis(grid, (jnp.arange(top)[None, :] + rotation) % top, axis=1)


def portions_of(amount, total, reach, lean, full):
    weights = [(1 << 20) // math.isqrt(grade ** lean) + 1 for grade in range(1, amount + 1)]
    largest = reach if full else min(reach, max(-(-total // amount), total * weights[0] // sum(weights)))
    least = 1 if total - largest >= amount - 1 else 0
    counts, rest = [largest] + [least] * (amount - 1), total - largest - least * (amount - 1)
    while rest > 0:
        movable = [i for i in range(1, amount) if counts[i] < largest] or [i for i in range(1, amount) if counts[i] < reach]
        pool, budget = sum([weights[i] for i in movable]), rest
        for i in movable:
            extra = min(reach - counts[i], max(1, budget * weights[i] // pool), rest)
            counts[i] = counts[i] + extra
            rest = rest - extra
    return np.array(counts)


def normal_values(own_key, extent, deviation, reach, shards=(), held_as=jnp.bfloat16):
    gain = level_of(own_key, extent, shards, -0.22, 0.18) if shards else 1.0
    values = jax.random.normal(own_key, extent, jnp.float32) * deviation * gain
    return jnp.minimum(jnp.maximum(values, -reach), reach).astype(held_as)


def setup_inputs(seed: int = 0, part: int = 0) -> dict:
    seeds = jax.random.split(jax.random.key(seed), 7)
    part_keys = jax.random.split(jax.random.fold_in(seeds[6], part), 7)
    tokens = normal_values(part_keys[0], (STEPS, ROWS, D), 1.0, 6.0, ((1, 16),))
    route_ids_keys = jax.random.split(jax.random.fold_in(part_keys[1], 1), STEPS * ROWS // ROWS_DEV)
    route_ids_turns = jax.random.permutation(jax.random.fold_in(part_keys[1], 3), STEPS * ROWS // ROWS_DEV)
    route_ids = jax.vmap(lambda own, number: deal_out(jax.random.fold_in(part_keys[1], 2), own, number, ROWS_DEV, EXPERTS, TOP, MOST, 2))(route_ids_keys, route_ids_turns).reshape((STEPS, ROWS, TOP))
    route_weight = jnp.clip(0.1 + 0.79999997 * jax.random.uniform(part_keys[2], (STEPS, ROWS, TOP), jnp.float32) ** level_of(part_keys[2], (STEPS, ROWS, TOP), ((1, 16),), -0.2, 0.2), 0.1, 0.9)
    gate_weight = normal_values(seeds[3], (D, EXPERTS * FF), D ** -0.5, 0.109375, ((1, 16),))
    up_weight = normal_values(seeds[4], (D, EXPERTS * FF), D ** -0.5, 0.109375, ((1, 16),))
    down_weight = normal_values(seeds[5], (EXPERTS * FF, D), FF ** -0.5, 0.0625, ((0, 16),))
    return dict(tokens=tokens, route_ids=route_ids, route_weight=route_weight, gate_weight=gate_weight, up_weight=up_weight, down_weight=down_weight)


def reference(tokens, route_ids, route_weight, gate_weight, up_weight, down_weight):
    group = N_HIDDEN // EXPERTS
    unit_dev = FF // group
    capacity = N_HIDDEN * MOST
    results = []
    for step_index in range(STEPS):
        rows_now = tokens[step_index]
        ids_now = route_ids[step_index]
        weight_now = route_weight[step_index]

        def one_expert(expert, total):
            expert = jnp.asarray(expert).astype(jnp.int32)
            matches = ids_now == expert
            picked = jnp.any(matches, axis=1)
            positions = jnp.nonzero(picked, size=capacity, fill_value=0)[0]
            valid = jnp.arange(capacity, dtype=jnp.int32) < jnp.sum(picked.astype(jnp.int32))
            chosen = rows_now[positions]
            start = (expert * FF).astype(jnp.int32)
            gate_cols = lax.dynamic_slice_in_dim(gate_weight, start, FF, 1)
            up_cols = lax.dynamic_slice_in_dim(up_weight, start, FF, 1)
            down_rows = lax.dynamic_slice_in_dim(down_weight, start, FF, 0)
            gate = jnp.dot(chosen, gate_cols, preferred_element_type=jnp.float32)
            upward = jnp.dot(chosen, up_cols, preferred_element_type=jnp.float32)
            hidden = (jax.nn.silu(gate) * upward).astype(jnp.bfloat16)
            hidden_blocks = hidden.reshape(capacity, group, unit_dev).astype(jnp.float32)
            down_blocks = down_rows.reshape(group, unit_dev, D).astype(jnp.float32)
            partial_value = jnp.einsum('cgu,gud->gcd', hidden_blocks, down_blocks).astype(jnp.bfloat16)
            expert_out = jnp.sum(partial_value.astype(jnp.float32), axis=0)
            shares = jnp.sum(jnp.where(matches, weight_now, 0.0), axis=1)
            factor = jnp.where(valid, shares[positions], 0.0)
            return total.at[positions].add(factor[:, None] * expert_out)

        start_total = jnp.zeros((ROWS, D), jnp.float32)
        total = lax.fori_loop(0, EXPERTS, one_expert, start_total)
        results.append(total.astype(jnp.bfloat16))
    return jnp.stack(results, axis=0)
```

```python
import functools

import jax
import jax.numpy as jnp
from jax import lax
from jax.experimental import pallas as pl
from jax.experimental.pallas import tpu as pltpu
from jax.sharding import PartitionSpec as P

EXPERTS = 8
MOST = 2
UNIT = 1024
WIDE = 512
SLOTS = 56
MESH = pl.DeviceIdType.MESH


def routing(ids, shares, steps, rows, experts, step_of, slot_of, row, owner_axis):
    shape = experts.shape
    before = jnp.zeros(shape, jnp.int32)
    picked = jnp.zeros(shape, jnp.int32)
    factor = jnp.zeros(shape, jnp.float32)
    for number in range(steps * rows):
        step, place = number // rows, number % rows
        first, second = ids[step, place, 0], ids[step, place, 1]
        named_first, named_second = experts == first, experts == second
        named = jnp.where(named_first | named_second, 1, 0)
        share = jnp.where(named_first, shares[step, place, 0], 0.0) + jnp.where(
            named_second, shares[step, place, 1], 0.0
        )
        here = row == number
        picked = jnp.where(here, named, picked)
        factor = jnp.where(here, share, factor)
        later = (row > number) & (row < (step + 1) * rows)
        before = before + jnp.where(later, named, 0)
    chosen = (picked == 1) & (before == slot_of) & (row // rows == step_of)
    return jnp.where(chosen, 1.0, 0.0), jnp.where(chosen, factor, 0.0)


def kernel(
    n,
    tokens,
    ids,
    shares,
    gate,
    up,
    down,
    out,
    send,
    near,
    far,
    staged,
    x,
    w,
    hidden,
    kept,
    give,
    take,
    sums,
    back,
    factors,
    w_sem,
    send_sem,
    near_sem,
    pass_sem,
    far_sem,
    give_sem,
    take_sem,
    sums_sem,
    back_sem,
    own_sem,
):
    steps, rows, width = tokens.shape
    units = gate.shape[1]
    chips = n // 2
    places = steps * MOST
    per_expert = chips // EXPERTS
    me = lax.axis_index("hidden")
    core, chip = lax.rem(me, 2), me // 2
    sibling = {"hidden": chip * 2 + (1 - core)}
    slots = w.shape[0]
    deep = width // UNIT
    blocks_up = units // WIDE
    first_units = 2 * deep * blocks_up
    down_rows = min(UNIT, units)
    down_deep = units // down_rows
    blocks_down = width // WIDE
    down_units = down_deep * blocks_down
    early = min(down_units, slots - first_units)

    def peer(distance):
        return lax.rem(chip + distance, chips)

    def device(other):
        return {"hidden": other * 2 + core}

    def up_copy(block, i, ref, base):
        slot = block * 2 * deep + base + i
        return pltpu.make_async_copy(
            ref.at[pl.ds(i * UNIT, UNIT), pl.ds(pl.multiple_of(block * WIDE, WIDE), WIDE)],
            w.at[slot],
            w_sem.at[slot],
        )

    def up_copies(block):
        return [up_copy(block, i, gate, 0) for i in range(deep)] + [
            up_copy(block, i, up, deep) for i in range(deep)
        ]

    def down_copy(number):
        block, i = number // down_deep, lax.rem(number, down_deep)
        slot = lax.rem(first_units + number, slots)
        return pltpu.make_async_copy(
            down.at[
                pl.ds(pl.multiple_of(i * down_rows, down_rows), down_rows),
                pl.ds(pl.multiple_of(block * WIDE, WIDE), WIDE),
            ],
            w.at[slot, pl.ds(0, down_rows), :],
            w_sem.at[slot],
        )

    barrier = pltpu.get_barrier_semaphore()

    def greet(distance, carry):
        pl.semaphore_signal(barrier, inc=1, device_id=device(peer(distance)), device_id_type=MESH)
        return carry

    lax.fori_loop(1, chips, greet, 0)
    pl.semaphore_signal(barrier, inc=1, device_id=sibling, device_id_type=MESH)

    def start_up(block, carry):
        for copy in up_copies(block):
            copy.start()
        return carry

    lax.fori_loop(0, blocks_up, start_up, 0)

    many = EXPERTS * places
    place = lax.broadcasted_iota(jnp.int32, (many, steps * rows), 0)
    row = lax.broadcasted_iota(jnp.int32, (many, steps * rows), 1)
    chooser, _ = routing(
        ids, shares, steps, rows, place // places, place % places // MOST, place % MOST, row, 1
    )
    owned = jnp.concatenate([tokens[step].astype(jnp.float32) for step in range(steps)], axis=0)
    packed = jnp.dot(chooser, owned, preferred_element_type=jnp.float32)
    for expert in range(EXPERTS):
        send[expert] = packed[expert * places : (expert + 1) * places].astype(jnp.bfloat16)

    pl.semaphore_wait(barrier, chips)

    def send_copy(distance):
        other = peer(distance)
        return pltpu.make_async_remote_copy(
            src_ref=send.at[other // per_expert],
            dst_ref=near.at[chip],
            send_sem=send_sem.at[other],
            recv_sem=near_sem.at[chip],
            device_id=device(other),
            device_id_type=MESH,
        )

    def arrival(source):
        return pltpu.make_async_remote_copy(
            src_ref=send.at[0],
            dst_ref=near.at[source],
            send_sem=send_sem.at[source],
            recv_sem=near_sem.at[source],
            device_id=device(source),
            device_id_type=MESH,
        )

    def pass_copy(source):
        return pltpu.make_async_remote_copy(
            src_ref=near.at[source],
            dst_ref=far.at[source],
            send_sem=pass_sem.at[source],
            recv_sem=far_sem.at[source],
            device_id=sibling,
            device_id_type=MESH,
        )

    def start_send(distance, carry):
        send_copy(distance).start()
        return carry

    lax.fori_loop(1, chips, start_send, 0)
    own = pltpu.make_async_copy(send.at[chip // per_expert], near.at[chip], own_sem)
    own.start()

    def start_down(number, carry):
        down_copy(number).start()
        return carry

    lax.fori_loop(0, early, start_down, 0)

    own.wait()
    pass_copy(chip).start()

    def forward(distance, carry):
        source = lax.rem(chip - distance + chips, chips)
        arrival(source).wait_recv()
        pass_copy(source).start()
        return carry

    lax.fori_loop(1, chips, forward, 0)

    count = chips * places
    row = lax.broadcasted_iota(jnp.int32, (steps * rows, count), 0)
    place = lax.broadcasted_iota(jnp.int32, (steps * rows, count), 1)
    _, found = routing(
        ids,
        shares,
        steps,
        rows,
        place // (places * per_expert),
        place % places // MOST,
        place % MOST,
        row,
        0,
    )
    factors[...] = found

    pairs = 8 // places

    def stage_near(group, carry):
        staged[group] = jnp.concatenate(
            [near[group * pairs + i].astype(jnp.float32) for i in range(pairs)], axis=0
        )
        return carry

    lax.fori_loop(0, chips // pairs, stage_near, 0)

    def await_far(source, carry):
        pass_copy(source).wait()
        return carry

    lax.fori_loop(0, chips, await_far, 0)

    def stage_far(group, carry):
        staged[chips // pairs + group] = jnp.concatenate(
            [far[group * pairs + i].astype(jnp.float32) for i in range(pairs)], axis=0
        )
        return carry

    lax.fori_loop(0, chips // pairs, stage_far, 0)
    x[...] = staged[...].reshape(x.shape).astype(jnp.bfloat16)

    def up_block(block, carry):
        copies = up_copies(block)
        base = block * 2 * deep
        for copy in copies[:deep]:
            copy.wait()
        gated = jnp.dot(
            x[...],
            w[pl.ds(base, deep)].reshape(width, WIDE),
            preferred_element_type=jnp.float32,
        )
        for copy in copies[deep:]:
            copy.wait()
        upward = jnp.dot(
            x[...],
            w[pl.ds(base + deep, deep)].reshape(width, WIDE),
            preferred_element_type=jnp.float32,
        )
        value = gated / (1.0 + jnp.exp(-gated)) * upward
        hidden[:, pl.ds(pl.multiple_of(block * WIDE, WIDE), WIDE)] = value.astype(jnp.bfloat16)
        for i in range(2 * deep):
            number = early + block * 2 * deep + i

            @pl.when(number < down_units)
            def _():
                down_copy(number).start()

        return carry

    lax.fori_loop(0, blocks_up, up_block, 0)

    half = chips * places

    def give_copy(block):
        return pltpu.make_async_remote_copy(
            src_ref=give.at[block],
            dst_ref=take.at[block],
            send_sem=give_sem.at[block],
            recv_sem=take_sem.at[block],
            device_id=sibling,
            device_id_type=MESH,
        )

    def back_copy(block, distance):
        other = peer(distance)
        return pltpu.make_async_remote_copy(
            src_ref=sums.at[block, other],
            dst_ref=back.at[block, chip],
            send_sem=sums_sem.at[block, other],
            recv_sem=back_sem.at[block, chip],
            device_id=device(other),
            device_id_type=MESH,
        )

    def back_arrival(block, source):
        return pltpu.make_async_remote_copy(
            src_ref=sums.at[block, source],
            dst_ref=back.at[block, source],
            send_sem=sums_sem.at[block, source],
            recv_sem=back_sem.at[block, source],
            device_id=device(source),
            device_id_type=MESH,
        )

    def compute(block):
        for i in range(down_deep):
            down_copy(block * down_deep + i).wait()
        slot = lax.rem(first_units + block * down_deep, slots)
        weights = w[pl.ds(slot, down_deep), pl.ds(0, down_rows), :].reshape(units, WIDE)
        partial = jnp.dot(hidden[...], weights, preferred_element_type=jnp.float32)
        kept[block] = partial[:half]
        give[block] = partial[half:].astype(jnp.bfloat16)
        give_copy(block).start()

    def exchange(block):
        give_copy(block).wait_recv()
        total = kept[block] + take[block].astype(jnp.float32)
        for other in range(chips):
            sums[block, other] = total[other * places : (other + 1) * places].astype(jnp.bfloat16)

        def start_back(distance, carry):
            back_copy(block, distance).start()
            return carry

        lax.fori_loop(1, chips, start_back, 0)
        back[block, chip] = sums[block, chip]

    def combine(block):
        def await_back(distance, carry):
            back_arrival(block, lax.rem(chip - distance + chips, chips)).wait_recv()
            return carry

        lax.fori_loop(1, chips, await_back, 0)
        pieces = jnp.concatenate(
            [back[block, source].astype(jnp.float32) for source in range(chips)], axis=0
        )
        mixed = jnp.dot(
            factors[...],
            pieces,
            preferred_element_type=jnp.float32,
            precision=lax.Precision.HIGHEST,
        )
        columns = pl.ds(pl.multiple_of(block * WIDE, WIDE), WIDE)
        for step in range(steps):
            out[step, :, columns] = mixed[step * rows : (step + 1) * rows]

    lag = 3

    def down_block(block, carry):
        compute(block)

        @pl.when(block >= 1)
        def _():
            exchange(block - 1)

        @pl.when(block >= lag)
        def _():
            combine(block - lag)

        return carry

    lax.fori_loop(0, blocks_down, down_block, 0)
    exchange(blocks_down - 1)

    def finish(block, carry):
        combine(block)
        return carry

    lax.fori_loop(blocks_down - lag, blocks_down, finish, 0)

    def settle_send(distance, carry):
        send_copy(distance).wait_send()
        return carry

    lax.fori_loop(1, chips, settle_send, 0)

    def settle_block(block, carry):
        give_copy(block).wait_send()

        def settle_back(distance, inner):
            back_copy(block, distance).wait_send()
            return inner

        return lax.fori_loop(1, chips, settle_back, carry)

    lax.fori_loop(0, blocks_down, settle_block, 0)


def on_device(tokens, route_ids, route_weight, gate_weight, up_weight, down_weight):
    n = lax.axis_size("hidden")
    chips = n // 2
    steps, rows, width = tokens.shape
    units = gate_weight.shape[1]
    places = steps * MOST
    half = chips * places
    blocks = width // WIDE
    down_rows = min(UNIT, units)
    total_units = 2 * (width // UNIT) * (units // WIDE) + (units // down_rows) * blocks
    slots = min(SLOTS, total_units)
    bf16, f32 = jnp.bfloat16, jnp.float32
    dma = pltpu.SemaphoreType.DMA
    mixed = pl.pallas_call(
        functools.partial(kernel, n),
        out_shape=jax.ShapeDtypeStruct((steps, rows, width), f32),
        in_specs=[
            pl.BlockSpec(memory_space=pltpu.VMEM),
            pl.BlockSpec(memory_space=pltpu.SMEM),
            pl.BlockSpec(memory_space=pltpu.SMEM),
            pl.BlockSpec(memory_space=pl.ANY),
            pl.BlockSpec(memory_space=pl.ANY),
            pl.BlockSpec(memory_space=pl.ANY),
        ],
        out_specs=pl.BlockSpec(memory_space=pltpu.VMEM),
        scratch_shapes=[
            pltpu.VMEM((EXPERTS, places, width), bf16),
            pltpu.VMEM((chips, places, width), bf16),
            pltpu.VMEM((chips, places, width), bf16),
            pltpu.VMEM((2 * half // 8, 8, width), f32),
            pltpu.VMEM((2 * half, width), bf16),
            pltpu.VMEM((slots, UNIT, WIDE), bf16),
            pltpu.VMEM((2 * half, units), bf16),
            pltpu.VMEM((blocks, half, WIDE), f32),
            pltpu.VMEM((blocks, half, WIDE), bf16),
            pltpu.VMEM((blocks, half, WIDE), bf16),
            pltpu.VMEM((blocks, chips, places, WIDE), bf16),
            pltpu.VMEM((blocks, chips, places, WIDE), bf16),
            pltpu.VMEM((steps * rows, half), f32),
            dma((slots,)),
            dma((chips,)),
            dma((chips,)),
            dma((chips,)),
            dma((chips,)),
            dma((blocks,)),
            dma((blocks,)),
            dma((blocks, chips)),
            dma((blocks, chips)),
            dma,
        ],
        compiler_params=pltpu.CompilerParams(
            collective_id=0, has_side_effects=True, vmem_limit_bytes=64 * 1024 * 1024
        ),
        cost_estimate=pl.CostEstimate(
            flops=12 * half * width * units, bytes_accessed=6 * width * units, transcendentals=0
        ),
    )(tokens, route_ids, route_weight, gate_weight, up_weight, down_weight)
    return mixed.astype(bf16)


def solution(mesh):
    placed = (
        P(None, ("parts", "hidden"), None),
        P(None, ("parts", "hidden"), None),
        P(None, ("parts", "hidden"), None),
        P(None, "hidden"),
        P(None, "hidden"),
        P("hidden", None),
    )
    return jax.shard_map(
        on_device,
        mesh=mesh,
        in_specs=placed,
        out_specs=P(None, ("parts", "hidden"), None),
        check_vma=False,
    )
```

```python
import functools

import jax
import jax.numpy as jnp
from jax import lax
from jax.experimental import pallas as pl
from jax.experimental.pallas import tpu as pltpu
from jax.sharding import PartitionSpec as P

EXPERTS = 8
MOST = 2
UNIT = 1024
WIDE = 1024
PART = 512
FED = 128
SLOTS = 28
MESH = pl.DeviceIdType.MESH


def routing(ids, shares, rows, place_expert, place_step, place_slot):
    steps = ids.shape[0]
    shape = place_expert.shape

    def along(ref, choice):
        return jnp.concatenate([ref[step, choice : choice + 1, :] for step in range(steps)], axis=1)

    named_first = along(ids, 0) == place_expert
    named_second = along(ids, 1) == place_expert
    picked = jnp.where(named_first | named_second, 1.0, 0.0)
    earlier = lax.broadcasted_iota(jnp.int32, (shape[1], shape[1]), 0)
    later = lax.broadcasted_iota(jnp.int32, (shape[1], shape[1]), 1)
    ahead = jnp.where((earlier < later) & (earlier // rows == later // rows), 1.0, 0.0)
    before = jnp.dot(picked, ahead, preferred_element_type=jnp.float32)
    row = lax.broadcasted_iota(jnp.int32, shape, 1)
    same = (row // rows == place_step) & (before == place_slot.astype(jnp.float32))
    chosen = jnp.where(same, picked, 0.0)
    share = jnp.where(named_first, along(shares, 0), 0.0) + jnp.where(
        named_second, along(shares, 1), 0.0
    )
    return chosen, chosen * share


def product(rows, weights):
    return jnp.dot(rows, weights, preferred_element_type=jnp.float32)


def kernel(
    n,
    tokens_in,
    ids_in,
    shares_in,
    gate,
    up,
    down,
    out,
    tokens,
    ids,
    shares,
    send,
    near,
    far,
    staged,
    x,
    w,
    hidden,
    kept,
    give,
    take,
    sums,
    back,
    factors,
    w_sem,
    send_sem,
    near_sem,
    pass_sem,
    far_sem,
    give_sem,
    take_sem,
    sums_sem,
    back_sem,
    own_sem,
    in_sem,
):
    steps, rows, width = tokens.shape
    units = gate.shape[1]
    wide = min(WIDE, units)
    chips = n // 2
    places = steps * MOST
    per_expert = chips // EXPERTS
    me = lax.axis_index("hidden")
    core, chip = lax.rem(me, 2), me // 2
    sibling = {"hidden": chip * 2 + (1 - core)}
    slots = w.shape[0]
    deep = width // UNIT
    blocks_up = units // wide
    first_units = 2 * deep * blocks_up
    down_rows = min(UNIT, units)
    down_deep = units // down_rows
    blocks_down = width // WIDE
    parts = WIDE // PART
    down_units = down_deep * blocks_down
    early = min(down_units, slots - first_units)

    def peer(distance):
        other, bit = 0, 1
        while bit < chips:
            other = other + bit * lax.rem(chip // bit + distance // bit, 2)
            bit = 2 * bit
        return other

    def device(other):
        return {"hidden": other * 2 + core}

    def up_copy(block, i, ref, base):
        slot = block * 2 * deep + base + i
        return pltpu.make_async_copy(
            ref.at[pl.ds(i * UNIT, UNIT), pl.ds(pl.multiple_of(block * wide, wide), wide)],
            w.at[slot, :, pl.ds(0, wide)],
            w_sem.at[slot],
        )

    def up_copies(block):
        return [up_copy(block, i, gate, 0) for i in range(deep)] + [
            up_copy(block, i, up, deep) for i in range(deep)
        ]

    def down_copy(number):
        block, i = number // down_deep, lax.rem(number, down_deep)
        slot = lax.rem(first_units + number, slots)
        return pltpu.make_async_copy(
            down.at[
                pl.ds(pl.multiple_of(i * down_rows, down_rows), down_rows),
                pl.ds(pl.multiple_of(block * WIDE, WIDE), WIDE),
            ],
            w.at[slot, pl.ds(0, down_rows), :],
            w_sem.at[slot],
        )

    barrier = pltpu.get_barrier_semaphore()

    def greet(distance, carry):
        pl.semaphore_signal(barrier, inc=1, device_id=device(peer(distance)), device_id_type=MESH)
        return carry

    def farthest_first(step):
        lax.fori_loop(0, chips - 1, lambda i, carry: step(chips - 1 - i, carry), 0)

    farthest_first(greet)
    pl.semaphore_signal(barrier, inc=1, device_id=sibling, device_id_type=MESH)
    inputs = [
        pltpu.make_async_copy(source, target, in_sem.at[i])
        for i, (source, target) in enumerate(
            [(ids_in, ids), (shares_in, shares), (tokens_in, tokens)]
        )
    ]
    for copy in inputs:
        copy.start()

    def start_up(block, carry):
        for copy in up_copies(block):
            copy.start()
        return carry

    lax.fori_loop(0, blocks_up, start_up, 0)

    for copy in inputs:
        copy.wait()
    place = lax.broadcasted_iota(jnp.int32, (EXPERTS * places, steps * rows), 0)
    chooser, _ = routing(
        ids, shares, rows, place // places, place % places // MOST, place % MOST
    )
    owned = jnp.concatenate([tokens[step].astype(jnp.float32) for step in range(steps)], axis=0)
    packed = jnp.dot(chooser, owned, preferred_element_type=jnp.float32)
    for expert in range(EXPERTS):
        send[expert] = packed[expert * places : (expert + 1) * places].astype(jnp.bfloat16)

    pl.semaphore_wait(barrier, chips)

    def send_copy(distance):
        other = peer(distance)
        return pltpu.make_async_remote_copy(
            src_ref=send.at[other // per_expert],
            dst_ref=near.at[chip],
            send_sem=send_sem.at[other],
            recv_sem=near_sem.at[chip],
            device_id=device(other),
            device_id_type=MESH,
        )

    def arrival(source):
        return pltpu.make_async_remote_copy(
            src_ref=send.at[0],
            dst_ref=near.at[source],
            send_sem=send_sem.at[source],
            recv_sem=near_sem.at[source],
            device_id=device(source),
            device_id_type=MESH,
        )

    def pass_copy(source):
        return pltpu.make_async_remote_copy(
            src_ref=near.at[source],
            dst_ref=far.at[source],
            send_sem=pass_sem.at[source],
            recv_sem=far_sem.at[source],
            device_id=sibling,
            device_id_type=MESH,
        )

    def start_send(distance, carry):
        send_copy(distance).start()
        return carry

    farthest_first(start_send)
    own = pltpu.make_async_copy(send.at[chip // per_expert], near.at[chip], own_sem)
    own.start()

    def start_down(number, carry):
        down_copy(number).start()
        return carry

    lax.fori_loop(0, early, start_down, 0)

    own.wait()
    pass_copy(chip).start()

    def forward(distance, carry):
        source = peer(distance)
        arrival(source).wait_recv()
        pass_copy(source).start()
        return carry

    lax.fori_loop(1, chips, forward, 0)

    place = lax.broadcasted_iota(jnp.int32, (chips * places, steps * rows), 0)
    _, found = routing(
        ids,
        shares,
        rows,
        place // (places * per_expert),
        place % places // MOST,
        place % MOST,
    )
    factors[...] = found.T

    pairs = 8 // places

    def stage_near(group, carry):
        staged[group] = jnp.concatenate(
            [near[group * pairs + i].astype(jnp.float32) for i in range(pairs)], axis=0
        )
        return carry

    lax.fori_loop(0, chips // pairs, stage_near, 0)

    def await_far(source, carry):
        pass_copy(source).wait()
        return carry

    lax.fori_loop(0, chips, await_far, 0)

    def stage_far(group, carry):
        staged[chips // pairs + group] = jnp.concatenate(
            [far[group * pairs + i].astype(jnp.float32) for i in range(pairs)], axis=0
        )
        return carry

    lax.fori_loop(0, chips // pairs, stage_far, 0)
    held = 2 * chips * places
    x[pl.ds(0, held), :] = staged[...].reshape(held, width).astype(jnp.bfloat16)
    if x.shape[0] > held:
        x[pl.ds(held, x.shape[0] - held), :] = jnp.zeros((x.shape[0] - held, width), x.dtype)

    def up_block(block, carry):
        copies = up_copies(block)
        base = block * 2 * deep
        for copy in copies[:deep]:
            copy.wait()
        gated = product(x[...], w[pl.ds(base, deep), :, pl.ds(0, wide)].reshape(width, wide))
        for copy in copies[deep:]:
            copy.wait()
        upward = product(x[...], w[pl.ds(base + deep, deep), :, pl.ds(0, wide)].reshape(width, wide))
        value = gated / (1.0 + jnp.exp(-gated)) * upward
        hidden[:, pl.ds(pl.multiple_of(block * wide, wide), wide)] = value.astype(jnp.bfloat16)
        for i in range(2 * deep):
            number = early + block * 2 * deep + i

            @pl.when(number < down_units)
            def _():
                down_copy(number).start()

        return carry

    lax.fori_loop(0, blocks_up, up_block, 0)

    half = chips * places

    def give_copy(block):
        return pltpu.make_async_remote_copy(
            src_ref=give.at[block],
            dst_ref=take.at[block],
            send_sem=give_sem.at[block],
            recv_sem=take_sem.at[block],
            device_id=sibling,
            device_id_type=MESH,
        )

    def back_copy(block, distance):
        other = peer(distance)
        return pltpu.make_async_remote_copy(
            src_ref=sums.at[block, other],
            dst_ref=back.at[block, chip],
            send_sem=sums_sem.at[block, other],
            recv_sem=back_sem.at[block, chip],
            device_id=device(other),
            device_id_type=MESH,
        )

    def back_arrival(block, source):
        return pltpu.make_async_remote_copy(
            src_ref=sums.at[block, source],
            dst_ref=back.at[block, source],
            send_sem=sums_sem.at[block, source],
            recv_sem=back_sem.at[block, source],
            device_id=device(source),
            device_id_type=MESH,
        )

    def compute(group, part):
        block = group * parts + part
        if part == 0:
            for i in range(down_deep):
                down_copy(group * down_deep + i).wait()
        slot = lax.rem(first_units + group * down_deep, slots)
        weights = w[pl.ds(slot, down_deep), pl.ds(0, down_rows), pl.ds(part * PART, PART)]
        partial = product(hidden[...], weights.reshape(units, PART))
        kept[block] = partial[:half]
        give[block] = partial[half : 2 * half].astype(jnp.bfloat16)
        give_copy(block).start()

    def exchange(block):
        give_copy(block).wait_recv()
        total = kept[block] + take[block].astype(jnp.float32)
        for other in range(chips):
            sums[block, other] = total[other * places : (other + 1) * places].astype(jnp.bfloat16)

        def start_back(distance, carry):
            back_copy(block, distance).start()
            return carry

        farthest_first(start_back)
        back[block, chip] = sums[block, chip]

    def combine(block):
        def await_back(distance, carry):
            back_arrival(block, peer(distance)).wait_recv()
            return carry

        lax.fori_loop(1, chips, await_back, 0)
        pieces = jnp.concatenate(
            [back[block, source].astype(jnp.float32) for source in range(chips)], axis=0
        )
        mixed = jnp.dot(
            factors[...],
            pieces,
            preferred_element_type=jnp.float32,
            precision=lax.Precision.HIGHEST,
        )
        columns = pl.ds(pl.multiple_of(block * PART, PART), PART)
        for step in range(steps):
            out[step, :, columns] = mixed[step * rows : (step + 1) * rows]

    lag = min(4, blocks_down * parts)

    def down_group(group, carry):
        for part in range(parts):
            block = group * parts + part
            compute(group, part)

            @pl.when(block >= 1)
            def _():
                exchange(block - 1)

            @pl.when(block >= lag)
            def _():
                combine(block - lag)

        return carry

    lax.fori_loop(0, blocks_down, down_group, 0)
    exchange(blocks_down * parts - 1)

    def finish(block, carry):
        combine(block)
        return carry

    lax.fori_loop(blocks_down * parts - lag, blocks_down * parts, finish, 0)

    def settle_send(distance, carry):
        send_copy(distance).wait_send()
        return carry

    lax.fori_loop(1, chips, settle_send, 0)

    def settle_block(block, carry):
        give_copy(block).wait_send()

        def settle_back(distance, inner):
            back_copy(block, distance).wait_send()
            return inner

        return lax.fori_loop(1, chips, settle_back, carry)

    lax.fori_loop(0, blocks_down * parts, settle_block, 0)


def on_device(tokens, route_ids, route_weight, gate_weight, up_weight, down_weight):
    n = lax.axis_size("hidden")
    chips = n // 2
    steps, rows, width = tokens.shape
    units = gate_weight.shape[1]
    choices = route_ids.shape[2]
    places = steps * MOST
    half = chips * places
    blocks = width // PART
    down_rows = min(UNIT, units)
    wide = min(WIDE, units)
    total_units = 2 * (width // UNIT) * (units // wide) + (units // down_rows) * (width // WIDE)
    fed = max(FED, 2 * half)
    slots = min(SLOTS, total_units)
    bf16, f32 = jnp.bfloat16, jnp.float32
    dma = pltpu.SemaphoreType.DMA
    mixed = pl.pallas_call(
        functools.partial(kernel, n),
        out_shape=jax.ShapeDtypeStruct((steps, rows, width), f32),
        in_specs=[
            pl.BlockSpec(memory_space=pl.ANY),
            pl.BlockSpec(memory_space=pl.ANY),
            pl.BlockSpec(memory_space=pl.ANY),
            pl.BlockSpec(memory_space=pl.ANY),
            pl.BlockSpec(memory_space=pl.ANY),
            pl.BlockSpec(memory_space=pl.ANY),
        ],
        out_specs=pl.BlockSpec(memory_space=pltpu.VMEM),
        scratch_shapes=[
            pltpu.VMEM((steps, rows, width), bf16),
            pltpu.VMEM((steps, choices, rows), jnp.int32),
            pltpu.VMEM((steps, choices, rows), f32),
            pltpu.VMEM((EXPERTS, places, width), bf16),
            pltpu.VMEM((chips, places, width), bf16),
            pltpu.VMEM((chips, places, width), bf16),
            pltpu.VMEM((2 * half // 8, 8, width), f32),
            pltpu.VMEM((fed, width), bf16),
            pltpu.VMEM((slots, UNIT, WIDE), bf16),
            pltpu.VMEM((fed, units), bf16),
            pltpu.VMEM((blocks, half, PART), f32),
            pltpu.VMEM((blocks, half, PART), bf16),
            pltpu.VMEM((blocks, half, PART), bf16),
            pltpu.VMEM((blocks, chips, places, PART), bf16),
            pltpu.VMEM((blocks, chips, places, PART), bf16),
            pltpu.VMEM((steps * rows, half), f32),
            dma((slots,)),
            dma((chips,)),
            dma((chips,)),
            dma((chips,)),
            dma((chips,)),
            dma((blocks,)),
            dma((blocks,)),
            dma((blocks, chips)),
            dma((blocks, chips)),
            dma,
            dma((3,)),
        ],
        compiler_params=pltpu.CompilerParams(
            collective_id=0, has_side_effects=True, vmem_limit_bytes=64 * 1024 * 1024
        ),
        cost_estimate=pl.CostEstimate(
            flops=12 * half * width * units, bytes_accessed=6 * width * units, transcendentals=0
        ),
    )(tokens, route_ids.swapaxes(1, 2), route_weight.swapaxes(1, 2), gate_weight, up_weight, down_weight)
    return mixed.astype(bf16)


def solution(mesh):
    placed = (
        P(None, ("parts", "hidden"), None),
        P(None, ("parts", "hidden"), None),
        P(None, ("parts", "hidden"), None),
        P(None, "hidden"),
        P(None, "hidden"),
        P("hidden", None),
    )
    return jax.shard_map(
        on_device,
        mesh=mesh,
        in_specs=placed,
        out_specs=P(None, ("parts", "hidden"), None),
        check_vma=False,
    )
```

```python
import functools

import jax
import jax.numpy as jnp
from jax import lax
from jax.experimental import pallas as pl
from jax.experimental.pallas import tpu as pltpu
from jax.sharding import PartitionSpec as P

EXPERTS = 8
MOST = 2
UNIT = 1024
WIDE = 1024
PART = 512
FED = 128
SLOTS = 28
MESH = pl.DeviceIdType.MESH


def routing(ids, shares, rows, place_expert, place_step, place_slot):
    steps = ids.shape[0]
    shape = place_expert.shape

    def along(ref, choice):
        return jnp.concatenate([ref[step, choice : choice + 1, :] for step in range(steps)], axis=1)

    named_first = along(ids, 0) == place_expert
    named_second = along(ids, 1) == place_expert
    picked = jnp.where(named_first | named_second, 1.0, 0.0)
    earlier = lax.broadcasted_iota(jnp.int32, (shape[1], shape[1]), 0)
    later = lax.broadcasted_iota(jnp.int32, (shape[1], shape[1]), 1)
    ahead = jnp.where((earlier < later) & (earlier // rows == later // rows), 1.0, 0.0)
    before = jnp.dot(picked, ahead, preferred_element_type=jnp.float32)
    row = lax.broadcasted_iota(jnp.int32, shape, 1)
    same = (row // rows == place_step) & (before == place_slot.astype(jnp.float32))
    chosen = jnp.where(same, picked, 0.0)
    share = jnp.where(named_first, along(shares, 0), 0.0) + jnp.where(
        named_second, along(shares, 1), 0.0
    )
    return chosen, chosen * share


def product(rows, weights):
    return jnp.dot(rows, weights, preferred_element_type=jnp.float32)


def kernel(
    n,
    tokens_in,
    ids_in,
    shares_in,
    gate,
    up,
    down,
    out,
    tokens,
    ids,
    shares,
    send,
    near,
    far,
    staged,
    x,
    w,
    hidden,
    kept,
    give,
    take,
    sums,
    back,
    factors,
    w_sem,
    send_sem,
    near_sem,
    pass_sem,
    far_sem,
    give_sem,
    take_sem,
    sums_sem,
    back_sem,
    own_sem,
    in_sem,
):
    steps, rows, width = tokens.shape
    units = gate.shape[1]
    wide = min(WIDE, units)
    chips = n // 2
    places = steps * MOST
    per_expert = chips // EXPERTS
    me = lax.axis_index("hidden")
    core, chip = lax.rem(me, 2), me // 2
    sibling = {"hidden": chip * 2 + (1 - core)}
    slots = w.shape[0]
    deep = width // UNIT
    blocks_up = units // wide
    first_units = 2 * deep * blocks_up
    down_rows = min(UNIT, units)
    down_deep = units // down_rows
    blocks_down = width // WIDE
    parts = WIDE // PART
    down_units = down_deep * blocks_down
    early = min(down_units, slots - first_units) // down_deep

    def peer(distance):
        other, bit = 0, 1
        while bit < chips:
            other = other + bit * lax.rem(chip // bit + distance // bit, 2)
            bit = 2 * bit
        return other

    def device(other):
        return {"hidden": other * 2 + core}

    def up_copy(block, i, ref, base):
        slot = block * 2 * deep + base + i
        return pltpu.make_async_copy(
            ref.at[pl.ds(i * UNIT, UNIT), pl.ds(pl.multiple_of(block * wide, wide), wide)],
            w.at[slot, :, pl.ds(0, wide)],
            w_sem.at[slot, 0],
        )

    def up_copies(block):
        return [up_copy(block, i, gate, 0) for i in range(deep)] + [
            up_copy(block, i, up, deep) for i in range(deep)
        ]

    def down_copy(number, part):
        group, i = number // down_deep, lax.rem(number, down_deep)
        slot = lax.rem(first_units + number, slots)
        return pltpu.make_async_copy(
            down.at[
                pl.ds(pl.multiple_of(i * down_rows, down_rows), down_rows),
                pl.ds(pl.multiple_of(group * WIDE + part * PART, PART), PART),
            ],
            w.at[slot, pl.ds(0, down_rows), pl.ds(part * PART, PART)],
            w_sem.at[slot, part],
        )

    def start_group(group):
        for part in range(parts):
            for i in range(down_deep):
                down_copy(group * down_deep + i, part).start()

    barrier = pltpu.get_barrier_semaphore()

    def greet(distance, carry):
        pl.semaphore_signal(barrier, inc=1, device_id=device(peer(distance)), device_id_type=MESH)
        return carry

    def farthest_first(step):
        lax.fori_loop(0, chips - 1, lambda i, carry: step(chips - 1 - i, carry), 0)

    farthest_first(greet)
    pl.semaphore_signal(barrier, inc=1, device_id=sibling, device_id_type=MESH)
    inputs = [
        pltpu.make_async_copy(source, target, in_sem.at[i])
        for i, (source, target) in enumerate(
            [(ids_in, ids), (shares_in, shares), (tokens_in, tokens)]
        )
    ]
    for copy in inputs:
        copy.start()

    def start_up(block, carry):
        for copy in up_copies(block):
            copy.start()
        return carry

    lax.fori_loop(0, blocks_up, start_up, 0)

    for copy in inputs:
        copy.wait()
    place = lax.broadcasted_iota(jnp.int32, (EXPERTS * places, steps * rows), 0)
    chooser, _ = routing(
        ids, shares, rows, place // places, place % places // MOST, place % MOST
    )
    owned = jnp.concatenate([tokens[step].astype(jnp.float32) for step in range(steps)], axis=0)
    packed = jnp.dot(chooser, owned, preferred_element_type=jnp.float32)
    for expert in range(EXPERTS):
        send[expert] = packed[expert * places : (expert + 1) * places].astype(jnp.bfloat16)

    held = 2 * chips * places
    if x.shape[0] > held:
        x[pl.ds(held, x.shape[0] - held), :] = jnp.zeros((x.shape[0] - held, width), x.dtype)

    pl.semaphore_wait(barrier, chips)

    def send_copy(distance):
        other = peer(distance)
        return pltpu.make_async_remote_copy(
            src_ref=send.at[other // per_expert],
            dst_ref=near.at[chip],
            send_sem=send_sem.at[other],
            recv_sem=near_sem.at[chip],
            device_id=device(other),
            device_id_type=MESH,
        )

    def arrival(source):
        return pltpu.make_async_remote_copy(
            src_ref=send.at[0],
            dst_ref=near.at[source],
            send_sem=send_sem.at[source],
            recv_sem=near_sem.at[source],
            device_id=device(source),
            device_id_type=MESH,
        )

    def pass_copy(source):
        return pltpu.make_async_remote_copy(
            src_ref=near.at[source],
            dst_ref=far.at[source],
            send_sem=pass_sem.at[source],
            recv_sem=far_sem.at[source],
            device_id=sibling,
            device_id_type=MESH,
        )

    def start_send(distance, carry):
        send_copy(distance).start()
        return carry

    farthest_first(start_send)
    own = pltpu.make_async_copy(send.at[chip // per_expert], near.at[chip], own_sem)
    own.start()

    def start_down(group, carry):
        start_group(group)
        return carry

    lax.fori_loop(0, early, start_down, 0)

    own.wait()
    pass_copy(chip).start()

    def forward(distance, carry):
        source = peer(distance)
        arrival(source).wait_recv()
        pass_copy(source).start()
        return carry

    lax.fori_loop(1, chips, forward, 0)

    place = lax.broadcasted_iota(jnp.int32, (chips * places, steps * rows), 0)
    _, found = routing(
        ids,
        shares,
        rows,
        place // (places * per_expert),
        place % places // MOST,
        place % MOST,
    )
    factors[...] = found.T

    pairs = 8 // places

    def stage_near(group, carry):
        staged[group] = jnp.concatenate(
            [near[group * pairs + i].astype(jnp.float32) for i in range(pairs)], axis=0
        )
        return carry

    lax.fori_loop(0, chips // pairs, stage_near, 0)

    def await_far(source, carry):
        pass_copy(source).wait()
        return carry

    lax.fori_loop(0, chips, await_far, 0)

    def stage_far(group, carry):
        staged[chips // pairs + group] = jnp.concatenate(
            [far[group * pairs + i].astype(jnp.float32) for i in range(pairs)], axis=0
        )
        return carry

    lax.fori_loop(0, chips // pairs, stage_far, 0)
    x[pl.ds(0, held), :] = staged[...].reshape(held, width).astype(jnp.bfloat16)

    def up_block(block, carry):
        copies = up_copies(block)
        base = block * 2 * deep
        for copy in copies:
            copy.wait()
        gated = product(x[...], w[pl.ds(base, deep), :, pl.ds(0, wide)].reshape(width, wide))
        upward = product(x[...], w[pl.ds(base + deep, deep), :, pl.ds(0, wide)].reshape(width, wide))
        value = gated / (1.0 + jnp.exp(-gated)) * upward
        hidden[:, pl.ds(pl.multiple_of(block * wide, wide), wide)] = value.astype(jnp.bfloat16)
        first = block * 2 * deep // down_deep
        last = (block + 1) * 2 * deep // down_deep
        for i in range(-(-2 * deep // down_deep)):

            @pl.when((first + i < last) & (early + first + i < blocks_down))
            def _():
                start_group(early + first + i)

        return carry

    lax.fori_loop(0, blocks_up, up_block, 0)

    half = chips * places

    def give_copy(block):
        return pltpu.make_async_remote_copy(
            src_ref=give.at[block],
            dst_ref=take.at[block],
            send_sem=give_sem.at[block],
            recv_sem=take_sem.at[block],
            device_id=sibling,
            device_id_type=MESH,
        )

    def back_copy(block, distance):
        other = peer(distance)
        return pltpu.make_async_remote_copy(
            src_ref=sums.at[block, other],
            dst_ref=back.at[block, chip],
            send_sem=sums_sem.at[block, other],
            recv_sem=back_sem.at[block, chip],
            device_id=device(other),
            device_id_type=MESH,
        )

    def back_arrival(block, source):
        return pltpu.make_async_remote_copy(
            src_ref=sums.at[block, source],
            dst_ref=back.at[block, source],
            send_sem=sums_sem.at[block, source],
            recv_sem=back_sem.at[block, source],
            device_id=device(source),
            device_id_type=MESH,
        )

    def compute(group, part):
        block = group * parts + part
        for i in range(down_deep):
            down_copy(group * down_deep + i, part).wait()
        slot = lax.rem(first_units + group * down_deep, slots)
        weights = w[pl.ds(slot, down_deep), pl.ds(0, down_rows), pl.ds(part * PART, PART)]
        partial = product(hidden[...], weights.reshape(units, PART))
        kept[block] = partial[:half]
        give[block] = partial[half : 2 * half].astype(jnp.bfloat16)
        give_copy(block).start()

    def exchange(block):
        give_copy(block).wait_recv()
        total = kept[block] + take[block].astype(jnp.float32)
        for other in range(chips):
            sums[block, other] = total[other * places : (other + 1) * places].astype(jnp.bfloat16)

        def start_back(distance, carry):
            back_copy(block, distance).start()
            return carry

        farthest_first(start_back)
        back[block, chip] = sums[block, chip]

    def combine(block):
        def await_back(distance, carry):
            back_arrival(block, peer(distance)).wait_recv()
            return carry

        lax.fori_loop(1, chips, await_back, 0)
        pieces = jnp.concatenate(
            [back[block, source].astype(jnp.float32) for source in range(chips)], axis=0
        )
        mixed = jnp.dot(
            factors[...],
            pieces,
            preferred_element_type=jnp.float32,
            precision=lax.Precision.HIGHEST,
        )
        columns = pl.ds(pl.multiple_of(block * PART, PART), PART)
        for step in range(steps):
            out[step, :, columns] = mixed[step * rows : (step + 1) * rows]

    lag = min(4, blocks_down * parts)

    def down_group(group, carry):
        for part in range(parts):
            block = group * parts + part
            compute(group, part)

            @pl.when(block >= 1)
            def _():
                exchange(block - 1)

            @pl.when(block >= lag)
            def _():
                combine(block - lag)

        return carry

    lax.fori_loop(0, blocks_down, down_group, 0)
    final = blocks_down * parts - 1
    exchange(final)

    def settle_send(distance, carry):
        send_copy(distance).wait_send()
        return carry

    lax.fori_loop(1, chips, settle_send, 0)

    def settle_block(block, carry):
        give_copy(block).wait_send()

        def settle_back(distance, inner):
            back_copy(block, distance).wait_send()
            return inner

        return lax.fori_loop(1, chips, settle_back, carry)

    lax.fori_loop(0, final, settle_block, 0)

    def finish(block, carry):
        combine(block)
        return carry

    lax.fori_loop(final + 1 - lag, final, finish, 0)
    settle_block(final, 0)
    combine(final)


def on_device(tokens, route_ids, route_weight, gate_weight, up_weight, down_weight):
    n = lax.axis_size("hidden")
    chips = n // 2
    steps, rows, width = tokens.shape
    units = gate_weight.shape[1]
    choices = route_ids.shape[2]
    places = steps * MOST
    half = chips * places
    blocks = width // PART
    down_rows = min(UNIT, units)
    wide = min(WIDE, units)
    total_units = 2 * (width // UNIT) * (units // wide) + (units // down_rows) * (width // WIDE)
    fed = max(FED, 2 * half)
    slots = min(SLOTS, total_units)
    bf16, f32 = jnp.bfloat16, jnp.float32
    dma = pltpu.SemaphoreType.DMA
    mixed = pl.pallas_call(
        functools.partial(kernel, n),
        out_shape=pltpu.VMEM((steps, rows, width), f32),
        in_specs=[
            pl.BlockSpec(memory_space=pl.ANY),
            pl.BlockSpec(memory_space=pl.ANY),
            pl.BlockSpec(memory_space=pl.ANY),
            pl.BlockSpec(memory_space=pl.ANY),
            pl.BlockSpec(memory_space=pl.ANY),
            pl.BlockSpec(memory_space=pl.ANY),
        ],
        out_specs=pl.BlockSpec(memory_space=pltpu.VMEM),
        scratch_shapes=[
            pltpu.VMEM((steps, rows, width), bf16),
            pltpu.VMEM((steps, choices, rows), jnp.int32),
            pltpu.VMEM((steps, choices, rows), f32),
            pltpu.VMEM((EXPERTS, places, width), bf16),
            pltpu.VMEM((chips, places, width), bf16),
            pltpu.VMEM((chips, places, width), bf16),
            pltpu.VMEM((2 * half // 8, 8, width), f32),
            pltpu.VMEM((fed, width), bf16),
            pltpu.VMEM((slots, UNIT, WIDE), bf16),
            pltpu.VMEM((fed, units), bf16),
            pltpu.VMEM((blocks, half, PART), f32),
            pltpu.VMEM((blocks, half, PART), bf16),
            pltpu.VMEM((blocks, half, PART), bf16),
            pltpu.VMEM((blocks, chips, places, PART), bf16),
            pltpu.VMEM((blocks, chips, places, PART), bf16),
            pltpu.VMEM((steps * rows, half), f32),
            dma((slots, WIDE // PART)),
            dma((chips,)),
            dma((chips,)),
            dma((chips,)),
            dma((chips,)),
            dma((blocks,)),
            dma((blocks,)),
            dma((blocks, chips)),
            dma((blocks, chips)),
            dma,
            dma((3,)),
        ],
        compiler_params=pltpu.CompilerParams(
            collective_id=0, has_side_effects=True, vmem_limit_bytes=66_600_000
        ),
        cost_estimate=pl.CostEstimate(
            flops=12 * half * width * units, bytes_accessed=6 * width * units, transcendentals=0
        ),
    )(tokens, route_ids.swapaxes(1, 2), route_weight.swapaxes(1, 2), gate_weight, up_weight, down_weight)
    return mixed.astype(bf16)


def solution(mesh):
    placed = (
        P(None, ("parts", "hidden"), None),
        P(None, ("parts", "hidden"), None),
        P(None, ("parts", "hidden"), None),
        P(None, "hidden"),
        P(None, "hidden"),
        P("hidden", None),
    )
    return jax.shard_map(
        on_device,
        mesh=mesh,
        in_specs=placed,
        out_specs=P(None, ("parts", "hidden"), None),
        check_vma=False,
    )
```

```python
import functools

import jax
import jax.numpy as jnp
from jax import lax
from jax.experimental import pallas as pl
from jax.experimental.pallas import tpu as pltpu
from jax.sharding import PartitionSpec as P

EXPERTS = 8
MOST = 2
UNIT = 1024
WIDE = 1024
PART = 512
FED = 128
SLOTS = 28
MESH = pl.DeviceIdType.MESH


def routing(ids, shares, rows, place_expert, place_step, place_slot):
    steps = ids.shape[0]
    shape = place_expert.shape

    def along(ref, choice):
        return jnp.concatenate([ref[step, choice : choice + 1, :] for step in range(steps)], axis=1)

    named_first = along(ids, 0) == place_expert
    named_second = along(ids, 1) == place_expert
    picked = jnp.where(named_first | named_second, 1.0, 0.0)
    earlier = lax.broadcasted_iota(jnp.int32, (shape[1], shape[1]), 0)
    later = lax.broadcasted_iota(jnp.int32, (shape[1], shape[1]), 1)
    ahead = jnp.where((earlier < later) & (earlier // rows == later // rows), 1.0, 0.0)
    before = jnp.dot(picked, ahead, preferred_element_type=jnp.float32)
    row = lax.broadcasted_iota(jnp.int32, shape, 1)
    same = (row // rows == place_step) & (before == place_slot.astype(jnp.float32))
    chosen = jnp.where(same, picked, 0.0)
    share = jnp.where(named_first, along(shares, 0), 0.0) + jnp.where(
        named_second, along(shares, 1), 0.0
    )
    return chosen, chosen * share


def product(rows, weights):
    return jnp.dot(rows, weights, preferred_element_type=jnp.float32)


def kernel(
    n,
    tokens_in,
    ids_in,
    shares_in,
    gate,
    up,
    down,
    out,
    tokens,
    ids,
    shares,
    send,
    near,
    far,
    staged,
    x,
    w,
    hidden,
    kept,
    give,
    take,
    sums,
    back,
    factors,
    w_sem,
    send_sem,
    near_sem,
    pass_sem,
    far_sem,
    give_sem,
    take_sem,
    sums_sem,
    back_sem,
    own_sem,
    in_sem,
):
    steps, rows, width = tokens.shape
    units = gate.shape[1]
    wide = min(WIDE, units)
    chips = n // 2
    places = steps * MOST
    per_expert = chips // EXPERTS
    me = lax.axis_index("hidden")
    core, chip = lax.rem(me, 2), me // 2
    sibling = {"hidden": chip * 2 + (1 - core)}
    slots = w.shape[0]
    deep = width // UNIT
    blocks_up = units // wide
    first_units = 2 * deep * blocks_up
    down_rows = min(UNIT, units)
    down_deep = units // down_rows
    blocks_down = width // WIDE
    parts = WIDE // PART
    down_units = down_deep * blocks_down
    early = min(down_units, slots - first_units) // down_deep

    def peer(distance):
        other, bit = 0, 1
        while bit < chips:
            other = other + bit * lax.rem(chip // bit + distance // bit, 2)
            bit = 2 * bit
        return other

    def device(other):
        return {"hidden": other * 2 + core}

    def up_copy(block, i, ref, base):
        slot = block * 2 * deep + base + i
        return pltpu.make_async_copy(
            ref.at[pl.ds(i * UNIT, UNIT), pl.ds(pl.multiple_of(block * wide, wide), wide)],
            w.at[slot, :, pl.ds(0, wide)],
            w_sem.at[slot, 0],
        )

    def up_copies(block):
        return [up_copy(block, i, gate, 0) for i in range(deep)] + [
            up_copy(block, i, up, deep) for i in range(deep)
        ]

    def down_copy(number, part):
        group, i = number // down_deep, lax.rem(number, down_deep)
        slot = lax.rem(first_units + number, slots)
        return pltpu.make_async_copy(
            down.at[
                pl.ds(pl.multiple_of(i * down_rows, down_rows), down_rows),
                pl.ds(pl.multiple_of(group * WIDE + part * PART, PART), PART),
            ],
            w.at[slot, pl.ds(0, down_rows), pl.ds(part * PART, PART)],
            w_sem.at[slot, part],
        )

    def start_group(group):
        for part in range(parts):
            for i in range(down_deep):
                down_copy(group * down_deep + i, part).start()

    barrier = pltpu.get_barrier_semaphore()

    def greet(distance, carry):
        pl.semaphore_signal(barrier, inc=1, device_id=device(peer(distance)), device_id_type=MESH)
        return carry

    def farthest_first(step):
        lax.fori_loop(0, chips - 1, lambda i, carry: step(chips - 1 - i, carry), 0)

    farthest_first(greet)
    pl.semaphore_signal(barrier, inc=1, device_id=sibling, device_id_type=MESH)
    inputs = [
        pltpu.make_async_copy(source, target, in_sem.at[i])
        for i, (source, target) in enumerate(
            [(ids_in, ids), (shares_in, shares), (tokens_in, tokens)]
        )
    ]
    for copy in inputs:
        copy.start()

    def start_up(block, carry):
        for copy in up_copies(block):
            copy.start()
        return carry

    lax.fori_loop(0, blocks_up, start_up, 0)

    for copy in inputs:
        copy.wait()
    place = lax.broadcasted_iota(jnp.int32, (EXPERTS * places, steps * rows), 0)
    chooser, _ = routing(
        ids, shares, rows, place // places, place % places // MOST, place % MOST
    )
    owned = jnp.concatenate([tokens[step].astype(jnp.float32) for step in range(steps)], axis=0)
    packed = jnp.dot(chooser, owned, preferred_element_type=jnp.float32)
    for expert in range(EXPERTS):
        send[expert] = packed[expert * places : (expert + 1) * places].astype(jnp.bfloat16)

    held = 2 * chips * places
    if x.shape[0] > held:
        x[pl.ds(held, x.shape[0] - held), :] = jnp.zeros((x.shape[0] - held, width), x.dtype)
        hidden[pl.ds(held, x.shape[0] - held), :] = jnp.zeros((x.shape[0] - held, units), x.dtype)

    pl.semaphore_wait(barrier, chips)

    def send_copy(distance):
        other = peer(distance)
        return pltpu.make_async_remote_copy(
            src_ref=send.at[other // per_expert],
            dst_ref=near.at[chip],
            send_sem=send_sem.at[other],
            recv_sem=near_sem.at[chip],
            device_id=device(other),
            device_id_type=MESH,
        )

    def arrival(source):
        return pltpu.make_async_remote_copy(
            src_ref=send.at[0],
            dst_ref=near.at[source],
            send_sem=send_sem.at[source],
            recv_sem=near_sem.at[source],
            device_id=device(source),
            device_id_type=MESH,
        )

    def pass_copy(source):
        return pltpu.make_async_remote_copy(
            src_ref=near.at[source],
            dst_ref=far.at[source],
            send_sem=pass_sem.at[source],
            recv_sem=far_sem.at[source],
            device_id=sibling,
            device_id_type=MESH,
        )

    def start_send(distance, carry):
        send_copy(distance).start()
        return carry

    farthest_first(start_send)
    own = pltpu.make_async_copy(send.at[chip // per_expert], near.at[chip], own_sem)
    own.start()

    def start_down(group, carry):
        start_group(group)
        return carry

    lax.fori_loop(0, early, start_down, 0)

    own.wait()
    pass_copy(chip).start()

    def forward(distance, carry):
        source = peer(distance)
        arrival(source).wait_recv()
        pass_copy(source).start()
        return carry

    lax.fori_loop(1, chips, forward, 0)

    place = lax.broadcasted_iota(jnp.int32, (chips * places, steps * rows), 0)
    _, found = routing(
        ids,
        shares,
        rows,
        place // (places * per_expert),
        place % places // MOST,
        place % MOST,
    )
    factors[...] = found.T

    pairs = 8 // places

    def stage_near(group, carry):
        staged[group] = jnp.concatenate(
            [near[group * pairs + i].astype(jnp.float32) for i in range(pairs)], axis=0
        )
        return carry

    lax.fori_loop(0, chips // pairs, stage_near, 0)

    def await_far(source, carry):
        pass_copy(source).wait()
        return carry

    lax.fori_loop(0, chips, await_far, 0)

    def stage_far(group, carry):
        staged[chips // pairs + group] = jnp.concatenate(
            [far[group * pairs + i].astype(jnp.float32) for i in range(pairs)], axis=0
        )
        return carry

    lax.fori_loop(0, chips // pairs, stage_far, 0)
    x[pl.ds(0, held), :] = staged[...].reshape(held, width).astype(jnp.bfloat16)

    def up_block(block, carry):
        copies = up_copies(block)
        base = block * 2 * deep
        for copy in copies:
            copy.wait()
        gated = product(x[...], w[pl.ds(base, deep), :, pl.ds(0, wide)].reshape(width, wide))
        upward = product(x[...], w[pl.ds(base + deep, deep), :, pl.ds(0, wide)].reshape(width, wide))
        gated, upward = gated[:held], upward[:held]
        value = gated / (1.0 + jnp.exp(-gated)) * upward
        hidden[pl.ds(0, held), pl.ds(pl.multiple_of(block * wide, wide), wide)] = value.astype(jnp.bfloat16)
        first = block * 2 * deep // down_deep
        last = (block + 1) * 2 * deep // down_deep
        for i in range(-(-2 * deep // down_deep)):

            @pl.when((first + i < last) & (early + first + i < blocks_down))
            def _():
                start_group(early + first + i)

        return carry

    lax.fori_loop(0, blocks_up, up_block, 0)

    half = chips * places

    def give_copy(block):
        return pltpu.make_async_remote_copy(
            src_ref=give.at[block],
            dst_ref=take.at[block],
            send_sem=give_sem.at[block],
            recv_sem=take_sem.at[block],
            device_id=sibling,
            device_id_type=MESH,
        )

    def back_copy(block, distance):
        other = peer(distance)
        return pltpu.make_async_remote_copy(
            src_ref=sums.at[block, other],
            dst_ref=back.at[block, chip],
            send_sem=sums_sem.at[block, other],
            recv_sem=back_sem.at[block, chip],
            device_id=device(other),
            device_id_type=MESH,
        )

    def back_arrival(block, source):
        return pltpu.make_async_remote_copy(
            src_ref=sums.at[block, source],
            dst_ref=back.at[block, source],
            send_sem=sums_sem.at[block, source],
            recv_sem=back_sem.at[block, source],
            device_id=device(source),
            device_id_type=MESH,
        )

    def compute(group, part):
        block = group * parts + part
        for i in range(down_deep):
            down_copy(group * down_deep + i, part).wait()
        slot = lax.rem(first_units + group * down_deep, slots)
        weights = w[pl.ds(slot, down_deep), pl.ds(0, down_rows), pl.ds(part * PART, PART)]
        partial = product(hidden[...], weights.reshape(units, PART))
        kept[block] = partial[:half]
        give[block] = partial[half : 2 * half].astype(jnp.bfloat16)
        give_copy(block).start()

    def exchange(block):
        give_copy(block).wait_recv()
        total = kept[block] + take[block].astype(jnp.float32)
        for other in range(chips):
            sums[block, other] = total[other * places : (other + 1) * places].astype(jnp.bfloat16)

        def start_back(distance, carry):
            back_copy(block, distance).start()
            return carry

        farthest_first(start_back)
        back[block, chip] = sums[block, chip]

    def combine(block):
        def await_back(distance, carry):
            back_arrival(block, peer(distance)).wait_recv()
            return carry

        lax.fori_loop(1, chips, await_back, 0)
        pieces = jnp.concatenate(
            [back[block, source].astype(jnp.float32) for source in range(chips)], axis=0
        )
        mixed = jnp.dot(
            factors[...],
            pieces,
            preferred_element_type=jnp.float32,
            precision=lax.Precision.HIGHEST,
        )
        columns = pl.ds(pl.multiple_of(block * PART, PART), PART)
        for step in range(steps):
            out[step, :, columns] = mixed[step * rows : (step + 1) * rows]

    lag = min(4, blocks_down * parts)

    def down_group(group, carry):
        for part in range(parts):
            block = group * parts + part
            compute(group, part)

            @pl.when(block >= 1)
            def _():
                exchange(block - 1)

            @pl.when(block >= lag)
            def _():
                combine(block - lag)

        return carry

    lax.fori_loop(0, blocks_down, down_group, 0)
    final = blocks_down * parts - 1
    exchange(final)

    def settle_send(distance, carry):
        send_copy(distance).wait_send()
        return carry

    lax.fori_loop(1, chips, settle_send, 0)

    def settle_block(block, carry):
        give_copy(block).wait_send()

        def settle_back(distance, inner):
            back_copy(block, distance).wait_send()
            return inner

        return lax.fori_loop(1, chips, settle_back, carry)

    lax.fori_loop(0, final, settle_block, 0)

    def finish(block, carry):
        combine(block)
        return carry

    lax.fori_loop(final + 1 - lag, final, finish, 0)
    settle_block(final, 0)
    combine(final)


def on_device(tokens, route_ids, route_weight, gate_weight, up_weight, down_weight):
    n = lax.axis_size("hidden")
    chips = n // 2
    steps, rows, width = tokens.shape
    units = gate_weight.shape[1]
    choices = route_ids.shape[2]
    places = steps * MOST
    half = chips * places
    blocks = width // PART
    down_rows = min(UNIT, units)
    wide = min(WIDE, units)
    total_units = 2 * (width // UNIT) * (units // wide) + (units // down_rows) * (width // WIDE)
    fed = max(FED, 2 * half)
    slots = min(SLOTS, total_units)
    bf16, f32 = jnp.bfloat16, jnp.float32
    dma = pltpu.SemaphoreType.DMA
    mixed = pl.pallas_call(
        functools.partial(kernel, n),
        out_shape=pltpu.VMEM((steps, rows, width), f32),
        in_specs=[
            pl.BlockSpec(memory_space=pl.ANY),
            pl.BlockSpec(memory_space=pl.ANY),
            pl.BlockSpec(memory_space=pl.ANY),
            pl.BlockSpec(memory_space=pl.ANY),
            pl.BlockSpec(memory_space=pl.ANY),
            pl.BlockSpec(memory_space=pl.ANY),
        ],
        out_specs=pl.BlockSpec(memory_space=pltpu.VMEM),
        scratch_shapes=[
            pltpu.VMEM((steps, rows, width), bf16),
            pltpu.VMEM((steps, choices, rows), jnp.int32),
            pltpu.VMEM((steps, choices, rows), f32),
            pltpu.VMEM((EXPERTS, places, width), bf16),
            pltpu.VMEM((chips, places, width), bf16),
            pltpu.VMEM((chips, places, width), bf16),
            pltpu.VMEM((2 * half // 8, 8, width), f32),
            pltpu.VMEM((fed, width), bf16),
            pltpu.VMEM((slots, UNIT, WIDE), bf16),
            pltpu.VMEM((fed, units), bf16),
            pltpu.VMEM((blocks, half, PART), f32),
            pltpu.VMEM((blocks, half, PART), bf16),
            pltpu.VMEM((blocks, half, PART), bf16),
            pltpu.VMEM((blocks, chips, places, PART), bf16),
            pltpu.VMEM((blocks, chips, places, PART), bf16),
            pltpu.VMEM((steps * rows, half), f32),
            dma((slots, WIDE // PART)),
            dma((chips,)),
            dma((chips,)),
            dma((chips,)),
            dma((chips,)),
            dma((blocks,)),
            dma((blocks,)),
            dma((blocks, chips)),
            dma((blocks, chips)),
            dma,
            dma((3,)),
        ],
        compiler_params=pltpu.CompilerParams(
            collective_id=0, has_side_effects=True, vmem_limit_bytes=66_600_000
        ),
        cost_estimate=pl.CostEstimate(
            flops=12 * half * width * units, bytes_accessed=6 * width * units, transcendentals=0
        ),
    )(tokens, route_ids.swapaxes(1, 2), route_weight.swapaxes(1, 2), gate_weight, up_weight, down_weight)
    return mixed.astype(bf16)


def solution(mesh):
    placed = (
        P(None, ("parts", "hidden"), None),
        P(None, ("parts", "hidden"), None),
        P(None, ("parts", "hidden"), None),
        P(None, "hidden"),
        P(None, "hidden"),
        P("hidden", None),
    )
    return jax.shard_map(
        on_device,
        mesh=mesh,
        in_specs=placed,
        out_specs=P(None, ("parts", "hidden"), None),
        check_vma=False,
    )
```
